32 devices in a mesh: space: 8 (over z, x), snap: 4 (over y, core).
Axes of the slice: x: 2, y: 2, z: 4, core: 2. Of those that a mesh axis runs over, the one named last changes fastest.
Arguments:
- velocity: bfloat16 [64, 3, 64, 32, 128], P('snap', None, 'space'), may hold values from -40 to 40
- phase_bins: int32 [64], replicated, may hold values from 0 to 23, as said below
- tile_owner: int32 [8], replicated, may hold values from 0 to 7, each once
Outputs:
- gram_tiles: float32 [8, 8, 64], P('space', None, 'snap')
The draws below stay inside these ranges and needn't reach their ends.
Inputs may be any that keep to these rules, and one draw needn't show every extreme that they name: `phase_bins`: every bin holds at least one snapshot. `tile_owner`: each tile has exactly one owner.
All inputs are finite; a program needn't handle non-finite values.
Results may differ from the reference program's by a relative error of at most 0.0003.
Values may be sent and summed in bfloat16 or wider, within the bound.
A program may use at most 128 MiB of HBM per device.

```python
import math
import jax
import jax.numpy as jnp
from jax import lax

NY = 32
NZ = 128
NB = 24
S = 64
NX = 64
NT = 8
NVOX = 262144


event_rate = 1.0 / 1024.0


event_low = 8.0


event_ratio = 38.0 / 8.0


def common_bins(key):
    key_draw = jax.random.fold_in(key, 101)
    key_cover = jax.random.fold_in(key, 202)
    raw_value = jax.random.randint(key_draw, (S,), 0, NB * NB, dtype=jnp.int32)
    levels = jnp.arange(1, NB, dtype=jnp.int32)
    bins_drawn = jnp.sum((levels[None, :] * levels[None, :] <= raw_value[:, None]).astype(jnp.int32), axis=1)
    chosen = jax.random.permutation(key_cover, S)[:NB]
    return bins_drawn.at[chosen].set(jnp.arange(NB, dtype=jnp.int32))


def draw_phase_bins(key, part):
    return common_bins(key)


def draw_velocity(key, part):
    bins_all = common_bins(key)
    key_phase = jax.random.fold_in(key, 303)
    key_amp = jax.random.fold_in(key, 404)
    key_mode = jax.random.fold_in(key, 505)
    key_frame = jax.random.fold_in(key, 606)
    phase_shapes = 0.8 * jax.random.normal(key_phase, (2, 3, NX, NY, NZ), jnp.float32)
    mode_shapes = jax.random.normal(key_mode, (4, 3, NX, NY, NZ), jnp.float32)
    amplitude = 0.3 * jax.random.normal(key_amp, (S, 4), jnp.float32)

    def one_frame(index):
        angle = 2.0 * math.pi * bins_all[index].astype(jnp.float32) / NB
        frame_key = jax.random.fold_in(key_frame, index)
        key_noise = jax.random.fold_in(frame_key, 1)
        key_spot = jax.random.fold_in(frame_key, 2)
        key_sign = jax.random.fold_in(frame_key, 3)
        shape = (3, NX, NY, NZ)
        noise_part = 0.5 * jax.random.normal(key_noise, shape, jnp.float32)
        spot = jax.random.uniform(key_spot, shape, jnp.float32)
        sign_draw = jax.random.normal(key_sign, shape, jnp.float32)
        fraction = jnp.minimum(spot / event_rate, 1.0)
        magnitude = event_low * jnp.exp(fraction * math.log(event_ratio))
        events = jnp.where(spot < event_rate, jnp.where(sign_draw < 0.0, -magnitude, magnitude), 0.0)
        row = amplitude[index]
        coherent = row[0] * mode_shapes[0] + row[1] * mode_shapes[1]
        coherent = coherent + row[2] * mode_shapes[2] + row[3] * mode_shapes[3]
        locked = jnp.cos(angle) * phase_shapes[0] + jnp.sin(angle) * phase_shapes[1]
        field_value = locked + coherent + noise_part + events
        return jnp.clip(field_value, -40.0, 40.0).astype(jnp.bfloat16)
    return lax.map(one_frame, jnp.arange(S, dtype=jnp.int32))


def setup_inputs(seed: int = 0) -> dict:
    key_of = jax.random.split(jax.random.key(seed), 4)
    velocity = draw_velocity(jax.random.fold_in(key_of[3], 71), 0)
    phase_bins = draw_phase_bins(jax.random.fold_in(key_of[3], 71), 0)
    tile_owner = jax.random.permutation(key_of[2], NT).astype(jnp.int32)
    return {"velocity": velocity, "phase_bins": phase_bins, "tile_owner": tile_owner}


def widen(field_in, direction):
    widths = [(0, 0)] * field_in.ndim
    widths[direction] = (2, 2)
    return jnp.pad(field_in, widths)


def derivative(padded_field, direction):
    length = padded_field.shape[direction] - 4

    def window_at(offset):
        return lax.slice_in_dim(padded_field, offset, offset + length, axis=direction)

    return (8.0 * (window_at(3) - window_at(1)) - (window_at(4) - window_at(0))) / 12.0


def curl_field(u_field, v_field, w_field, v_wide, w_wide, first):
    second = first + 1
    third = first + 2
    omega_x = derivative(widen(w_field, second), second) - derivative(widen(v_field, third), third)
    omega_y = derivative(widen(u_field, third), third) - derivative(w_wide, first)
    omega_z = derivative(v_wide, first) - derivative(widen(u_field, second), second)
    return jnp.stack([omega_x, omega_y, omega_z], axis=first)


def reference(velocity, phase_bins, tile_owner):
    def one_snapshot(frame):
        frame_float = frame.astype(jnp.float32)
        v_wide = widen(frame_float[1], 0)
        w_wide = widen(frame_float[2], 0)
        return curl_field(frame_float[0], frame_float[1], frame_float[2], v_wide, w_wide, 0).astype(jnp.bfloat16)

    vortex = lax.map(one_snapshot, velocity)
    planes = jnp.transpose(vortex, (2, 0, 1, 3, 4)).reshape(NX, S, 3 * NY * NZ)
    onehot = (phase_bins[None, :] == jnp.arange(NB, dtype=jnp.int32)[:, None]).astype(jnp.bfloat16)
    bin_counts = jnp.sum(onehot.astype(jnp.float32), axis=1)

    def accumulate(running, voxel_plane):
        bin_sums = jnp.dot(onehot, voxel_plane, preferred_element_type=jnp.float32)
        bin_means = bin_sums / bin_counts[:, None]
        fluctuation = (voxel_plane.astype(jnp.float32) - jnp.take(bin_means, phase_bins, axis=0)).astype(jnp.bfloat16)
        product = lax.dot_general(fluctuation, fluctuation, (((1,), (1,)), ((), ())), preferred_element_type=jnp.float32)
        return running + product, None

    gram_sum, _ = lax.scan(accumulate, jnp.zeros((S, S), jnp.float32), planes)
    gram_sum = gram_sum / NVOX
    blocks = gram_sum.reshape(NT, S // NT, S)
    tile_ids = jnp.arange(NT, dtype=jnp.int32)
    inverse = jnp.sum(tile_ids[None, :] * (tile_owner[None, :] == tile_ids[:, None]).astype(jnp.int32), axis=1)
    return jnp.take(blocks, inverse, axis=0)
```

```python
import functools
import jax
import jax.numpy as jnp
from jax import lax
from jax.experimental import pallas as pl
from jax.experimental.pallas import tpu as pltpu
from jax.sharding import PartitionSpec as P

NB = 24
MESH = pl.DeviceIdType.MESH
F32 = jnp.float32
BF16 = jnp.bfloat16
HIGH = lax.Precision.HIGHEST


def iota2(shape, dim):
    return lax.broadcasted_iota(jnp.int32, shape, dim)


def stencil(step):
    plus = jnp.where(step == 1, 8.0, 0.0) - jnp.where(step == 2, 1.0, 0.0)
    minus = jnp.where(step == -1, 8.0, 0.0) - jnp.where(step == -2, 1.0, 0.0)
    return plus - minus


def kernel(
    n_space, n_snap, inv_voxels,
    owner_ref, bins_ref, vel_ref, out_ref,
    ext, uu, perm, band_y, band_z, omega, send, recv, mean_mat, gram, mail, rows_in, cols_out, cols_in,
    local_sem, halo_send, halo_recv, a2a_send, a2a_recv, row_send, row_recv, col_send, col_recv,
):
    snaps, _, nx, ny, nz = vel_ref.shape
    total = snaps * n_snap
    half = snaps * ny // 2
    rows = snaps * ny
    part = rows // n_snap
    y_part = ny // n_snap
    pairs = nx // 2
    tile_rows = total // n_space
    chunks = 3 * pairs
    si = lax.axis_index("space")
    ti = lax.axis_index("snap")

    load_vw = pltpu.make_async_copy(vel_ref.at[:, 1:3], ext.at[:, :, 2 : nx + 2], local_sem.at[0])
    load_u = pltpu.make_async_copy(vel_ref.at[:, 0], uu, local_sem.at[1])
    load_vw.start()
    load_u.start()

    barrier = pltpu.get_barrier_semaphore()
    for o in range(1, n_snap):
        pl.semaphore_signal(
            barrier, inc=1, device_id={"snap": lax.rem(ti + o, n_snap)}, device_id_type=MESH
        )
    for o in range(1, n_space):
        pl.semaphore_signal(
            barrier, inc=1, device_id={"space": lax.rem(si + o, n_space)}, device_id_type=MESH
        )

    r = iota2((rows, rows), 0)
    c = iota2((rows, rows), 1)
    perm[...] = jnp.where(c == (r % snaps) * ny + r // snaps, 1.0, 0.0).astype(BF16)
    r = iota2((half, half), 0)
    c = iota2((half, half), 1)
    band_y[...] = jnp.where(r // ny == c // ny, stencil(c - r), 0.0).astype(BF16)
    r = iota2((2 * nz, 2 * nz), 0)
    c = iota2((2 * nz, 2 * nz), 1)
    band_z[...] = jnp.where(r // nz == c // nz, stencil(r - c), 0.0).astype(BF16)

    onehot = jnp.where(bins_ref[...] == iota2((32, total), 0), 1.0, 0.0).astype(F32)
    same = lax.dot_general(
        onehot, onehot, (((0,), (0,)), ((), ())), preferred_element_type=F32
    )
    averaging = same / jnp.sum(same, axis=0, keepdims=True)
    mean_mat[...] = averaging.astype(BF16)
    gram[...] = jnp.zeros_like(gram)

    pl.semaphore_wait(barrier, n_snap + n_space - 2)

    def to_left():
        return pltpu.make_async_remote_copy(
            vel_ref.at[:, 1:3, 0:2], ext.at[:, :, nx + 2 : nx + 4],
            halo_send.at[0], halo_recv.at[0],
            device_id={"space": si - 1}, device_id_type=MESH,
        )

    def to_right():
        return pltpu.make_async_remote_copy(
            vel_ref.at[:, 1:3, nx - 2 : nx], ext.at[:, :, 0:2],
            halo_send.at[1], halo_recv.at[1],
            device_id={"space": si + 1}, device_id_type=MESH,
        )

    @pl.when(si > 0)
    def _():
        to_left().start()

    @pl.when(si < n_space - 1)
    def _():
        to_right().start()

    @pl.when(si == 0)
    def _():
        ext[:, :, 0:2] = jnp.zeros((snaps, 2, 2, ny, nz), BF16)

    @pl.when(si == n_space - 1)
    def _():
        ext[:, :, nx + 2 : nx + 4] = jnp.zeros((snaps, 2, 2, ny, nz), BF16)

    order = sorted(range(1, n_snap), key=lambda o: abs(o - n_snap // 2))

    def a2a(k, o):
        dst = lax.rem(ti + o, n_snap)
        return pltpu.make_async_remote_copy(
            send.at[k, pl.ds(pl.multiple_of(dst * part, part), part)],
            recv.at[k, ti],
            a2a_send.at[k, o - 1], a2a_recv.at[k, o - 1],
            device_id={"snap": dst}, device_id_type=MESH,
        )

    def ship(k):
        moved = jnp.dot(perm[...], omega[...], preferred_element_type=F32)
        send[k] = moved.astype(BF16)
        for o in order:
            a2a(k, o).start()
        recv[k, ti] = send[k, pl.ds(pl.multiple_of(ti * part, part), part)]

    h_snaps = snaps // 2

    def pair_vw(comp, x, h):
        s = slice(h * h_snaps, (h + 1) * h_snaps)
        return jnp.concatenate(
            [ext[s, comp, x + 2 + i].reshape(half, nz) for i in range(2)], axis=1
        )

    def pair_u(x, h):
        s = slice(h * h_snaps, (h + 1) * h_snaps)
        return jnp.concatenate([uu[s, x + i].reshape(half, nz) for i in range(2)], axis=1)

    def d1_pair(comp, x, h):
        s = slice(h * h_snaps, (h + 1) * h_snaps)
        f = [ext[s, comp, x + i].reshape(half, nz).astype(F32) for i in range(6)]
        return jnp.concatenate(
            [8.0 * (f[i + 3] - f[i + 1]) - (f[i + 4] - f[i]) for i in range(2)], axis=1
        )

    def d2(field):
        return jnp.dot(band_y[...], field, preferred_element_type=F32)

    def d3(field):
        return jnp.dot(field, band_z[...], preferred_element_type=F32)

    def put(h, value):
        omega[h * half : (h + 1) * half] = (value * (1.0 / 12.0)).astype(BF16)

    load_vw.wait()

    def first_component(p, _):
        for h in range(2):
            put(h, d2(pair_vw(1, 2 * p, h)) - d3(pair_vw(0, 2 * p, h)))
        ship(p)
        return 0

    lax.fori_loop(0, pairs, first_component, 0)
    load_u.wait()

    def other_components(k, x):
        for h in range(2):
            put(h, d3(pair_u(x, h)) - d1_pair(1, x, h))
        ship(k)
        for h in range(2):
            put(h, d1_pair(0, x, h) - d2(pair_u(x, h)))
        ship(k + 1)

    def inner(p, _):
        other_components(pairs + 2 * p, 2 * p + 2)
        return 0

    lax.fori_loop(0, pairs - 2, inner, 0)

    @pl.when(si < n_space - 1)
    def _():
        to_left().wait_recv()

    @pl.when(si > 0)
    def _():
        to_right().wait_recv()

    def outer(p, _):
        other_components(chunks - 4 + 2 * p, p * (nx - 2))
        return 0

    lax.fori_loop(0, 2, outer, 0)

    def accumulate(k, _):
        for o in order:
            a2a(k, o).wait_recv()
        columns = jnp.concatenate(
            [
                jnp.concatenate(
                    [recv[k, t, y * snaps : (y + 1) * snaps] for t in range(n_snap)], axis=0
                )
                for y in range(y_part)
            ],
            axis=1,
        )
        mean = jnp.dot(mean_mat[...], columns, preferred_element_type=F32)
        near = (columns.astype(F32) - mean).astype(BF16)
        gram[...] += lax.dot_general(
            near, near, (((1,), (1,)), ((), ())), preferred_element_type=F32
        )
        return 0

    lax.fori_loop(0, chunks, accumulate, 0)

    eye = jnp.where(iota2((total, total), 0) == iota2((total, total), 1), 1.0, 0.0)
    onehot = jnp.where(bins_ref[...] == iota2((32, total), 0), 1.0, 0.0).astype(F32)
    same = lax.dot_general(
        onehot, onehot, (((0,), (0,)), ((), ())), preferred_element_type=F32
    )
    centre = eye - same / jnp.sum(same, axis=0, keepdims=True)
    r = iota2((total, total), 0)
    c = iota2((total, total), 1)
    owners = jnp.zeros((total, total), jnp.int32)
    for t in range(n_space):
        owners = jnp.where(c // tile_rows == t, owner_ref[t], owners)
    place = jnp.where((r // tile_rows == owners) & (r % tile_rows == c % tile_rows), 1.0, 0.0)
    lines = jnp.dot(
        jnp.dot(place, centre, preferred_element_type=F32, precision=HIGH),
        gram[...], preferred_element_type=F32, precision=HIGH,
    )
    done = jnp.dot(lines, centre, preferred_element_type=F32, precision=HIGH) * inv_voxels
    mail[...] = jnp.zeros_like(mail)
    mail[:, 0:total] = done

    def row_copy(o):
        dst = lax.rem(si + o, n_space)
        return pltpu.make_async_remote_copy(
            mail.at[pl.ds(pl.multiple_of(dst * tile_rows, tile_rows), tile_rows)],
            rows_in.at[si], row_send.at[o - 1], row_recv.at[o - 1],
            device_id={"space": dst}, device_id_type=MESH,
        )

    for o in range(1, n_space):
        row_copy(o).start()
    rows_in[si] = mail[pl.ds(pl.multiple_of(si * tile_rows, tile_rows), tile_rows)]
    for o in range(1, n_space):
        row_copy(o).wait_recv()
    mine = jnp.sum(rows_in[...], axis=0)
    cols_out[...] = mine

    def col_copy(o):
        return pltpu.make_async_remote_copy(
            cols_out, cols_in.at[o - 1], col_send.at[o - 1], col_recv.at[o - 1],
            device_id={"snap": lax.rem(ti + o, n_snap)}, device_id_type=MESH,
        )

    for o in order:
        col_copy(o).start()
    for o in order:
        col_copy(o).wait_recv()
    out_ref[...] = mine + jnp.sum(cols_in[...], axis=0)

    def drain(k, _):
        for o in order:
            a2a(k, o).wait_send()
        return 0

    lax.fori_loop(0, chunks, drain, 0)

    @pl.when(si > 0)
    def _():
        to_left().wait_send()

    @pl.when(si < n_space - 1)
    def _():
        to_right().wait_send()

    for o in range(1, n_space):
        row_copy(o).wait_send()
    for o in order:
        col_copy(o).wait_send()


def per_device(velocity, phase_bins, tile_owner):
    n_space = lax.axis_size("space")
    n_snap = lax.axis_size("snap")
    snaps, _, nx, ny, nz = velocity.shape
    total = snaps * n_snap
    rows = snaps * ny
    part = rows // n_snap
    chunks = 3 * (nx // 2)
    tile_rows = total // n_space
    wide = -(-total // 128) * 128
    dma = pltpu.SemaphoreType.DMA
    summed = pl.pallas_call(
        functools.partial(kernel, n_space, n_snap, 1.0 / (n_space * nx * ny * nz)),
        out_shape=jax.ShapeDtypeStruct((tile_rows, wide), F32),
        in_specs=[
            pl.BlockSpec(memory_space=pltpu.SMEM),
            pl.BlockSpec(memory_space=pltpu.VMEM),
            pl.BlockSpec(memory_space=pl.ANY),
        ],
        out_specs=pl.BlockSpec(memory_space=pltpu.VMEM),
        scratch_shapes=[
            pltpu.VMEM((snaps, 2, nx + 4, ny, nz), BF16),
            pltpu.VMEM((snaps, nx, ny, nz), BF16),
            pltpu.VMEM((rows, rows), BF16),
            pltpu.VMEM((rows // 2, rows // 2), BF16),
            pltpu.VMEM((2 * nz, 2 * nz), BF16),
            pltpu.VMEM((rows, 2 * nz), BF16),
            pltpu.VMEM((chunks, rows, 2 * nz), BF16),
            pltpu.VMEM((chunks, n_snap, part, 2 * nz), BF16),
            pltpu.VMEM((total, total), BF16),
            pltpu.VMEM((total, total), F32),
            pltpu.VMEM((total, wide), F32),
            pltpu.VMEM((n_space, tile_rows, wide), F32),
            pltpu.VMEM((tile_rows, wide), F32),
            pltpu.VMEM((n_snap - 1, tile_rows, wide), F32),
            dma((2,)),
            dma((2,)),
            dma((2,)),
            dma((chunks, n_snap - 1)),
            dma((chunks, n_snap - 1)),
            dma((n_space - 1,)),
            dma((n_space - 1,)),
            dma((n_snap - 1,)),
            dma((n_snap - 1,)),
        ],
        compiler_params=pltpu.CompilerParams(
            collective_id=0, has_side_effects=True, vmem_limit_bytes=48 * 1024 * 1024
        ),
        cost_estimate=pl.CostEstimate(
            flops=4_000_000_000, bytes_accessed=4_000_000, transcendentals=0
        ),
    )(tile_owner, phase_bins.reshape(1, total), velocity)
    return lax.dynamic_slice_in_dim(summed, lax.axis_index("snap") * snaps, snaps, axis=1)[None]


def solution(mesh):
    return jax.shard_map(
        per_device,
        mesh=mesh,
        in_specs=(P("snap", None, "space", None, None), P(), P()),
        out_specs=P("space", None, "snap"),
        check_vma=False,
    )
```

```python
import functools
import jax
import jax.numpy as jnp
from jax import lax
from jax.experimental import pallas as pl
from jax.experimental.pallas import tpu as pltpu
from jax.sharding import PartitionSpec as P

NB = 24
MESH = pl.DeviceIdType.MESH
F32 = jnp.float32
BF16 = jnp.bfloat16
HIGH = lax.Precision.HIGHEST


def iota2(shape, dim):
    return lax.broadcasted_iota(jnp.int32, shape, dim)


def stencil(step):
    plus = jnp.where(step == 1, 8.0, 0.0) - jnp.where(step == 2, 1.0, 0.0)
    minus = jnp.where(step == -1, 8.0, 0.0) - jnp.where(step == -2, 1.0, 0.0)
    return plus - minus


def kernel(
    n_space, n_snap, inv_voxels,
    owner_hbm, bins_hbm, vel_ref, out_ref,
    owner_ref, bins_ref, ext, uu, perm, band_y, band_z, omega, send, recv, mean_mat, centre_mat, left_mat, gram, mail, rows_in, cols_out, cols_in,
    local_sem, halo_send, halo_recv, a2a_send, a2a_recv, row_send, row_recv, col_send, col_recv,
):
    snaps, _, nx, ny, nz = vel_ref.shape
    total = snaps * n_snap
    half = snaps * ny // 2
    rows = snaps * ny
    part = rows // n_snap
    y_part = ny // n_snap
    pairs = nx // 2
    tile_rows = total // n_space
    chunks = 3 * pairs
    si = lax.axis_index("space")
    ti = lax.axis_index("snap")

    load_vw = pltpu.make_async_copy(vel_ref.at[:, 1:3], ext.at[:, :, 2 : nx + 2], local_sem.at[0])
    load_u = pltpu.make_async_copy(vel_ref.at[:, 0], uu, local_sem.at[1])
    load_bins = pltpu.make_async_copy(bins_hbm, bins_ref, local_sem.at[2])
    load_owner = pltpu.make_async_copy(owner_hbm, owner_ref, local_sem.at[3])
    load_vw.start()
    load_u.start()
    load_bins.start()
    load_owner.start()

    barrier = pltpu.get_barrier_semaphore()
    for o in range(1, n_snap):
        pl.semaphore_signal(
            barrier, inc=1, device_id={"snap": lax.rem(ti + o, n_snap)}, device_id_type=MESH
        )
    for o in range(1, n_space):
        pl.semaphore_signal(
            barrier, inc=1, device_id={"space": lax.rem(si + o, n_space)}, device_id_type=MESH
        )

    c = iota2((1, rows), 1)
    moved_to = (c % ny) * snaps + c // ny
    perm[...] = jnp.where(iota2((rows, rows), 0) == moved_to, 1.0, 0.0).astype(BF16)

    def band(size, length):
        r = iota2((size, size), 0)
        c = iota2((size, size), 1)
        first = (iota2((1, size), 1) // length) * length
        return jnp.where((r >= first) & (r < first + length), stencil(r - c), 0.0)

    band_y[...] = (-band(half, ny)).astype(BF16)
    band_z[...] = band(2 * nz, nz).astype(BF16)
    gram[...] = jnp.zeros_like(gram)

    def to_left(comp):
        return pltpu.make_async_remote_copy(
            vel_ref.at[:, comp + 1, 0:2], ext.at[:, comp, nx + 2 : nx + 4],
            halo_send.at[0, comp], halo_recv.at[0, comp],
            device_id={"space": si - 1}, device_id_type=MESH,
        )

    def to_right(comp):
        return pltpu.make_async_remote_copy(
            vel_ref.at[:, comp + 1, nx - 2 : nx], ext.at[:, comp, 0:2],
            halo_send.at[1, comp], halo_recv.at[1, comp],
            device_id={"space": si + 1}, device_id_type=MESH,
        )

    @pl.when(si == 0)
    def _():
        ext[:, :, 0:2] = jnp.zeros((snaps, 2, 2, ny, nz), BF16)

    @pl.when(si == n_space - 1)
    def _():
        ext[:, :, nx + 2 : nx + 4] = jnp.zeros((snaps, 2, 2, ny, nz), BF16)

    order = sorted(range(1, n_snap), key=lambda o: abs(o - n_snap // 2))

    def a2a(k, o):
        dst = lax.rem(ti + o, n_snap)
        return pltpu.make_async_remote_copy(
            send.at[k, pl.ds(pl.multiple_of(dst * part, part), part)],
            recv.at[k, ti],
            a2a_send.at[k, o - 1], a2a_recv.at[k, o - 1],
            device_id={"snap": dst}, device_id_type=MESH,
        )

    def arrange(k):
        moved = jnp.dot(perm[...], omega[...], preferred_element_type=F32)
        send[k] = moved.astype(BF16)

    def ship(k):
        for o in order:
            a2a(k, o).start()
        recv[k, ti] = send[k, pl.ds(pl.multiple_of(ti * part, part), part)]

    h_snaps = snaps // 2

    def pair_vw(comp, x, h):
        s = slice(h * h_snaps, (h + 1) * h_snaps)
        return jnp.concatenate(
            [ext[s, comp, x + 2 + i].reshape(half, nz) for i in range(2)], axis=1
        )

    def pair_u(x, h):
        s = slice(h * h_snaps, (h + 1) * h_snaps)
        return jnp.concatenate([uu[s, x + i].reshape(half, nz) for i in range(2)], axis=1)

    def d1_pair(comp, x, h):
        s = slice(h * h_snaps, (h + 1) * h_snaps)
        f = [ext[s, comp, x + i].reshape(half, nz).astype(F32) for i in range(6)]
        return jnp.concatenate(
            [8.0 * (f[i + 3] - f[i + 1]) - (f[i + 4] - f[i]) for i in range(2)], axis=1
        )

    def d2(field):
        return jnp.dot(band_y[...], field, preferred_element_type=F32)

    def d3(field):
        return jnp.dot(field, band_z[...], preferred_element_type=F32)

    def put(h, value):
        omega[h * half : (h + 1) * half] = (value * (1.0 / 12.0)).astype(BF16)

    def make_x(k, x):
        for h in range(2):
            put(h, d2(pair_vw(1, x, h)) - d3(pair_vw(0, x, h)))
        arrange(k)

    def make_y(k, x):
        for h in range(2):
            put(h, d3(pair_u(x, h)) - d1_pair(1, x, h))
        arrange(k)

    def make_z(k, x):
        for h in range(2):
            put(h, d1_pair(0, x, h) - d2(pair_u(x, h)))
        arrange(k)

    load_vw.wait()
    make_x(0, 0)

    pl.semaphore_wait(barrier, n_snap + n_space - 2)
    for comp in (1, 0):
        @pl.when(si > 0)
        def _():
            to_left(comp).start()

        @pl.when(si < n_space - 1)
        def _():
            to_right(comp).start()

    ship(0)

    def x_step(p, _):
        make_x(p, 2 * p)
        ship(p)
        return 0

    lax.fori_loop(1, pairs, x_step, 0)
    load_u.wait()

    def inner(p, _):
        k = pairs + 2 * p
        make_y(k, 2 * p + 2)
        ship(k)
        make_z(k + 1, 2 * p + 2)
        ship(k + 1)
        return 0

    lax.fori_loop(0, pairs - 2, inner, 0)

    load_bins.wait()
    load_owner.wait()
    onehot = jnp.where(bins_ref[...] == iota2((32, total), 0), 1.0, 0.0).astype(F32)
    same = lax.dot_general(
        onehot, onehot, (((0,), (0,)), ((), ())), preferred_element_type=F32
    )
    averaging = same / jnp.sum(same, axis=0, keepdims=True)
    mean_mat[...] = averaging.astype(BF16)
    r = iota2((total, total), 0)
    c = iota2((total, total), 1)
    centre = jnp.where(r == c, 1.0, 0.0) - averaging
    centre_mat[...] = centre
    c1 = iota2((1, total), 1)
    tile = c1 // tile_rows
    first_row = jnp.zeros((1, total), jnp.int32)
    for t in range(n_space):
        first_row = jnp.where(tile == t, owner_ref[t] * tile_rows, first_row)
    place = jnp.where(r == first_row + c1 % tile_rows, inv_voxels, 0.0)
    left_mat[...] = jnp.dot(place, centre, preferred_element_type=F32, precision=HIGH)

    def accumulate(k, _):
        for o in order:
            a2a(k, o).wait_recv()
        columns = jnp.concatenate(
            [
                jnp.concatenate(
                    [recv[k, t, y * snaps : (y + 1) * snaps] for t in range(n_snap)], axis=0
                )
                for y in range(y_part)
            ],
            axis=1,
        )
        mean = jnp.dot(mean_mat[...], columns, preferred_element_type=F32)
        near = (columns.astype(F32) - mean).astype(BF16)
        gram[...] += lax.dot_general(
            near, near, (((1,), (1,)), ((), ())), preferred_element_type=F32
        )
        return 0

    def edges(comp, make, base):
        @pl.when(si < n_space - 1)
        def _():
            to_left(comp).wait_recv()

        @pl.when(si > 0)
        def _():
            to_right(comp).wait_recv()

        def side(p, _):
            make(base + p, p * (nx - 2))
            ship(base + p)
            return 0

        lax.fori_loop(0, 2, side, 0)

    lax.fori_loop(0, 2, accumulate, 0)
    edges(1, make_y, chunks - 4)
    lax.fori_loop(2, 4, accumulate, 0)
    edges(0, make_z, chunks - 2)
    lax.fori_loop(4, chunks, accumulate, 0)

    lines = jnp.dot(left_mat[...], gram[...], preferred_element_type=F32, precision=HIGH)
    done = jnp.dot(lines, centre_mat[...], preferred_element_type=F32, precision=HIGH)
    mail[...] = jnp.zeros_like(mail)
    mail[:, 0:total] = done

    def row_copy(o):
        dst = lax.rem(si + o, n_space)
        return pltpu.make_async_remote_copy(
            mail.at[pl.ds(pl.multiple_of(dst * tile_rows, tile_rows), tile_rows)],
            rows_in.at[si], row_send.at[o - 1], row_recv.at[o - 1],
            device_id={"space": dst}, device_id_type=MESH,
        )

    for o in range(1, n_space):
        row_copy(o).start()
    rows_in[si] = mail[pl.ds(pl.multiple_of(si * tile_rows, tile_rows), tile_rows)]
    for o in range(1, n_space):
        row_copy(o).wait_recv()
    mine = jnp.sum(rows_in[...], axis=0)
    cols_out[...] = mine

    def col_copy(o):
        return pltpu.make_async_remote_copy(
            cols_out, cols_in.at[o - 1], col_send.at[o - 1], col_recv.at[o - 1],
            device_id={"snap": lax.rem(ti + o, n_snap)}, device_id_type=MESH,
        )

    for o in order:
        col_copy(o).start()
    for o in order:
        col_copy(o).wait_recv()
    out_ref[...] = mine + jnp.sum(cols_in[...], axis=0)

    def drain(k, _):
        for o in order:
            a2a(k, o).wait_send()
        return 0

    lax.fori_loop(0, chunks, drain, 0)

    for comp in range(2):
        @pl.when(si > 0)
        def _():
            to_left(comp).wait_send()

        @pl.when(si < n_space - 1)
        def _():
            to_right(comp).wait_send()

    for o in range(1, n_space):
        row_copy(o).wait_send()
    for o in order:
        col_copy(o).wait_send()


def per_device(velocity, phase_bins, tile_owner):
    n_space = lax.axis_size("space")
    n_snap = lax.axis_size("snap")
    snaps, _, nx, ny, nz = velocity.shape
    total = snaps * n_snap
    rows = snaps * ny
    part = rows // n_snap
    chunks = 3 * (nx // 2)
    tile_rows = total // n_space
    wide = -(-total // 128) * 128
    dma = pltpu.SemaphoreType.DMA
    summed = pl.pallas_call(
        functools.partial(kernel, n_space, n_snap, 1.0 / (n_space * nx * ny * nz)),
        out_shape=jax.ShapeDtypeStruct((tile_rows, wide), F32),
        in_specs=[
            pl.BlockSpec(memory_space=pl.ANY),
            pl.BlockSpec(memory_space=pl.ANY),
            pl.BlockSpec(memory_space=pl.ANY),
        ],
        out_specs=pl.BlockSpec(memory_space=pltpu.VMEM),
        scratch_shapes=[
            pltpu.SMEM((n_space,), jnp.int32),
            pltpu.VMEM((1, total), jnp.int32),
            pltpu.VMEM((snaps, 2, nx + 4, ny, nz), BF16),
            pltpu.VMEM((snaps, nx, ny, nz), BF16),
            pltpu.VMEM((rows, rows), BF16),
            pltpu.VMEM((rows // 2, rows // 2), BF16),
            pltpu.VMEM((2 * nz, 2 * nz), BF16),
            pltpu.VMEM((rows, 2 * nz), BF16),
            pltpu.VMEM((chunks, rows, 2 * nz), BF16),
            pltpu.VMEM((chunks, n_snap, part, 2 * nz), BF16),
            pltpu.VMEM((total, total), BF16),
            pltpu.VMEM((total, total), F32),
            pltpu.VMEM((total, total), F32),
            pltpu.VMEM((total, total), F32),
            pltpu.VMEM((total, wide), F32),
            pltpu.VMEM((n_space, tile_rows, wide), F32),
            pltpu.VMEM((tile_rows, wide), F32),
            pltpu.VMEM((n_snap - 1, tile_rows, wide), F32),
            dma((4,)),
            dma((2, 2)),
            dma((2, 2)),
            dma((chunks, n_snap - 1)),
            dma((chunks, n_snap - 1)),
            dma((n_space - 1,)),
            dma((n_space - 1,)),
            dma((n_snap - 1,)),
            dma((n_snap - 1,)),
        ],
        compiler_params=pltpu.CompilerParams(
            collective_id=0, has_side_effects=True, vmem_limit_bytes=62 * 1024 * 1024
        ),
        cost_estimate=pl.CostEstimate(
            flops=4_000_000_000, bytes_accessed=4_000_000, transcendentals=0
        ),
    )(tile_owner, phase_bins.reshape(1, total), velocity)
    return lax.dynamic_slice_in_dim(summed, lax.axis_index("snap") * snaps, snaps, axis=1)[None]


def solution(mesh):
    return jax.shard_map(
        per_device,
        mesh=mesh,
        in_specs=(P("snap", None, "space", None, None), P(), P()),
        out_specs=P("space", None, "snap"),
        check_vma=False,
    )
```

```python
import functools
import jax
import jax.numpy as jnp
from jax import lax
from jax.experimental import pallas as pl
from jax.experimental.pallas import tpu as pltpu
from jax.sharding import PartitionSpec as P

NB = 24
MESH = pl.DeviceIdType.MESH
F32 = jnp.float32
BF16 = jnp.bfloat16
HIGH = lax.Precision.HIGHEST


def iota2(shape, dim):
    return lax.broadcasted_iota(jnp.int32, shape, dim)


def stencil(step):
    plus = jnp.where(step == 1, 8.0, 0.0) - jnp.where(step == 2, 1.0, 0.0)
    minus = jnp.where(step == -1, 8.0, 0.0) - jnp.where(step == -2, 1.0, 0.0)
    return plus - minus


def kernel(
    n_space, n_snap, inv_voxels,
    owner_hbm, bins_hbm, vel_ref, out_ref,
    owner_ref, bins_ref, ext, uu, perm, band_y, band_z, omega, send, recv, weights, mail, rows_in, cols_out, cols_in,
    local_sem, halo_send, halo_recv, a2a_send, a2a_recv, row_send, row_recv, col_send, col_recv,
):
    snaps, _, nx, ny, nz = vel_ref.shape
    total = snaps * n_snap
    half = snaps * ny // 2
    rows = snaps * ny
    part = rows // n_snap
    y_part = ny // n_snap
    pairs = nx // 2
    tile_rows = total // n_space
    chunks = 3 * pairs
    si = lax.axis_index("space")
    ti = lax.axis_index("snap")

    load_vw = pltpu.make_async_copy(vel_ref.at[:, 1:3], ext.at[:, :, 2 : nx + 2], local_sem.at[0])
    load_u = pltpu.make_async_copy(vel_ref.at[:, 0], uu, local_sem.at[1])
    load_bins = pltpu.make_async_copy(bins_hbm, bins_ref, local_sem.at[2])
    load_owner = pltpu.make_async_copy(owner_hbm, owner_ref, local_sem.at[3])
    load_vw.start()
    load_u.start()
    load_bins.start()
    load_owner.start()

    barrier = pltpu.get_barrier_semaphore()
    for o in range(1, n_snap):
        pl.semaphore_signal(
            barrier, inc=1, device_id={"snap": lax.rem(ti + o, n_snap)}, device_id_type=MESH
        )
    for o in range(1, n_space):
        pl.semaphore_signal(
            barrier, inc=1, device_id={"space": lax.rem(si + o, n_space)}, device_id_type=MESH
        )

    c = iota2((1, rows), 1)
    moved_to = (c % ny) * snaps + c // ny
    perm[...] = jnp.where(iota2((rows, rows), 0) == moved_to, 1.0, 0.0).astype(BF16)

    def band(size, length):
        r = iota2((size, size), 0)
        c = iota2((size, size), 1)
        first = (iota2((1, size), 1) // length) * length
        return jnp.where((r >= first) & (r < first + length), stencil(r - c), 0.0)

    band_y[...] = (-band(half, ny)).astype(BF16)
    band_z[...] = band(2 * nz, nz).astype(BF16)
    mail[...] = jnp.zeros_like(mail)

    def to_left(comp):
        return pltpu.make_async_remote_copy(
            vel_ref.at[:, comp + 1, 0:2], ext.at[:, comp, nx + 2 : nx + 4],
            halo_send.at[0, comp], halo_recv.at[0, comp],
            device_id={"space": si - 1}, device_id_type=MESH,
        )

    def to_right(comp):
        return pltpu.make_async_remote_copy(
            vel_ref.at[:, comp + 1, nx - 2 : nx], ext.at[:, comp, 0:2],
            halo_send.at[1, comp], halo_recv.at[1, comp],
            device_id={"space": si + 1}, device_id_type=MESH,
        )

    @pl.when(si == 0)
    def _():
        ext[:, :, 0:2] = jnp.zeros((snaps, 2, 2, ny, nz), BF16)

    @pl.when(si == n_space - 1)
    def _():
        ext[:, :, nx + 2 : nx + 4] = jnp.zeros((snaps, 2, 2, ny, nz), BF16)

    order = sorted(range(1, n_snap), key=lambda o: abs(o - n_snap // 2))

    def a2a(k, o):
        dst = lax.rem(ti + o, n_snap)
        return pltpu.make_async_remote_copy(
            send.at[k, pl.ds(pl.multiple_of(dst * part, part), part)],
            recv.at[k, ti],
            a2a_send.at[k, o - 1], a2a_recv.at[k, o - 1],
            device_id={"snap": dst}, device_id_type=MESH,
        )

    def arrange(k):
        moved = jnp.dot(perm[...], omega[...], preferred_element_type=F32)
        send[k] = moved.astype(BF16)

    def ship(k):
        for o in order:
            a2a(k, o).start()
        recv[k, ti] = send[k, pl.ds(pl.multiple_of(ti * part, part), part)]

    h_snaps = snaps // 2

    def pair_vw(comp, x, h):
        s = slice(h * h_snaps, (h + 1) * h_snaps)
        return jnp.concatenate(
            [ext[s, comp, x + 2 + i].reshape(half, nz) for i in range(2)], axis=1
        )

    def pair_u(x, h):
        s = slice(h * h_snaps, (h + 1) * h_snaps)
        return jnp.concatenate([uu[s, x + i].reshape(half, nz) for i in range(2)], axis=1)

    def d1_pair(comp, x, h):
        s = slice(h * h_snaps, (h + 1) * h_snaps)
        f = [ext[s, comp, x + i].reshape(half, nz).astype(F32) for i in range(6)]
        return jnp.concatenate(
            [8.0 * (f[i + 3] - f[i + 1]) - (f[i + 4] - f[i]) for i in range(2)], axis=1
        )

    def d2(field):
        return jnp.dot(band_y[...], field, preferred_element_type=F32)

    def d3(field):
        return jnp.dot(field, band_z[...], preferred_element_type=F32)

    def put(h, value):
        omega[h * half : (h + 1) * half] = (value * (1.0 / 12.0)).astype(BF16)

    def make_x(k, x):
        for h in range(2):
            put(h, d2(pair_vw(1, x, h)) - d3(pair_vw(0, x, h)))
        arrange(k)

    def make_y(k, x):
        for h in range(2):
            put(h, d3(pair_u(x, h)) - d1_pair(1, x, h))
        arrange(k)

    def make_z(k, x):
        for h in range(2):
            put(h, d1_pair(0, x, h) - d2(pair_u(x, h)))
        arrange(k)

    load_vw.wait()
    make_x(0, 0)

    pl.semaphore_wait(barrier, n_snap + n_space - 2)
    for comp in (1, 0):
        @pl.when(si > 0)
        def _():
            to_left(comp).start()

        @pl.when(si < n_space - 1)
        def _():
            to_right(comp).start()

    ship(0)

    def x_step(p, _):
        make_x(p, 2 * p)
        ship(p)
        return 0

    lax.fori_loop(1, pairs, x_step, 0)
    load_u.wait()

    def inner(p, _):
        k = pairs + 2 * p
        make_y(k, 2 * p + 2)
        ship(k)
        make_z(k + 1, 2 * p + 2)
        ship(k + 1)
        return 0

    lax.fori_loop(0, pairs - 2, inner, 0)

    load_bins.wait()
    load_owner.wait()
    onehot = jnp.where(bins_ref[...] == iota2((32, total), 0), 1.0, 0.0).astype(F32)
    same = lax.dot_general(
        onehot, onehot, (((0,), (0,)), ((), ())), preferred_element_type=F32
    )
    averaging = same / jnp.sum(same, axis=0, keepdims=True)
    r = iota2((total, total), 0)
    c = iota2((total, total), 1)
    centre = jnp.where(r == c, 1.0, 0.0) - averaging
    c1 = iota2((1, total), 1)
    tile = c1 // tile_rows
    first_row = jnp.zeros((1, total), jnp.int32)
    for t in range(n_space):
        first_row = jnp.where(tile == t, owner_ref[t] * tile_rows, first_row)
    place = jnp.where(r == first_row + c1 % tile_rows, 1.0, 0.0)
    rest = jnp.concatenate(
        [centre, jnp.dot(place, centre, preferred_element_type=F32, precision=HIGH)], axis=0
    )
    pieces = []
    for term in range(3):
        piece = rest.astype(BF16).astype(F32)
        pieces.append(piece)
        rest = rest - piece
    weights[...] = jnp.concatenate(pieces, axis=1).astype(BF16)

    def accumulate(k, _):
        for o in order:
            a2a(k, o).wait_recv()
        columns = jnp.concatenate(
            [
                jnp.concatenate(
                    [recv[k, t, y * snaps : (y + 1) * snaps] for t in range(n_snap)], axis=0
                )
                for y in range(y_part)
            ],
            axis=1,
        )
        near = jnp.dot(
            weights[...], jnp.concatenate([columns] * 3, axis=0), preferred_element_type=F32
        ).astype(BF16)
        mail[:, 0:total] += lax.dot_general(
            near[total:], near[:total], (((1,), (1,)), ((), ())), preferred_element_type=F32
        )
        return 0

    def edges(comp, make, base):
        @pl.when(si < n_space - 1)
        def _():
            to_left(comp).wait_recv()

        @pl.when(si > 0)
        def _():
            to_right(comp).wait_recv()

        def side(p, _):
            make(base + p, p * (nx - 2))
            ship(base + p)
            return 0

        lax.fori_loop(0, 2, side, 0)

    lax.fori_loop(0, 2, accumulate, 0)
    edges(1, make_y, chunks - 4)
    lax.fori_loop(2, 4, accumulate, 0)
    edges(0, make_z, chunks - 2)
    lax.fori_loop(4, chunks, accumulate, 0)

    def row_copy(o):
        dst = lax.rem(si + o, n_space)
        return pltpu.make_async_remote_copy(
            mail.at[pl.ds(pl.multiple_of(dst * tile_rows, tile_rows), tile_rows)],
            rows_in.at[si], row_send.at[o - 1], row_recv.at[o - 1],
            device_id={"space": dst}, device_id_type=MESH,
        )

    for o in sorted(range(1, n_space), key=lambda o: abs(o - n_space // 2)):
        row_copy(o).start()
    rows_in[si] = mail[pl.ds(pl.multiple_of(si * tile_rows, tile_rows), tile_rows)]
    for o in range(1, n_space):
        row_copy(o).wait_recv()
    mine = jnp.sum(rows_in[...], axis=0) * inv_voxels
    cols_out[...] = mine

    def col_copy(o):
        return pltpu.make_async_remote_copy(
            cols_out, cols_in.at[o - 1], col_send.at[o - 1], col_recv.at[o - 1],
            device_id={"snap": lax.rem(ti + o, n_snap)}, device_id_type=MESH,
        )

    for o in order:
        col_copy(o).start()
    for o in order:
        col_copy(o).wait_recv()
    summed = mine + jnp.sum(cols_in[...], axis=0)
    wide = summed.shape[1]
    turned = pltpu.roll(summed, lax.rem(wide - ti * snaps, wide), 1)
    out_ref[0] = turned[:, 0:snaps]

    def drain(k, _):
        for o in order:
            a2a(k, o).wait_send()
        return 0

    lax.fori_loop(0, chunks, drain, 0)

    for comp in range(2):
        @pl.when(si > 0)
        def _():
            to_left(comp).wait_send()

        @pl.when(si < n_space - 1)
        def _():
            to_right(comp).wait_send()

    for o in range(1, n_space):
        row_copy(o).wait_send()
    for o in order:
        col_copy(o).wait_send()


def per_device(velocity, phase_bins, tile_owner):
    n_space = lax.axis_size("space")
    n_snap = lax.axis_size("snap")
    snaps, _, nx, ny, nz = velocity.shape
    total = snaps * n_snap
    rows = snaps * ny
    part = rows // n_snap
    chunks = 3 * (nx // 2)
    tile_rows = total // n_space
    wide = -(-total // 128) * 128
    dma = pltpu.SemaphoreType.DMA
    return pl.pallas_call(
        functools.partial(kernel, n_space, n_snap, 1.0 / (n_space * nx * ny * nz)),
        out_shape=jax.ShapeDtypeStruct((1, tile_rows, snaps), F32),
        in_specs=[
            pl.BlockSpec(memory_space=pl.ANY),
            pl.BlockSpec(memory_space=pl.ANY),
            pl.BlockSpec(memory_space=pl.ANY),
        ],
        out_specs=pl.BlockSpec(memory_space=pltpu.VMEM),
        scratch_shapes=[
            pltpu.SMEM((n_space,), jnp.int32),
            pltpu.VMEM((1, total), jnp.int32),
            pltpu.VMEM((snaps, 2, nx + 4, ny, nz), BF16),
            pltpu.VMEM((snaps, nx, ny, nz), BF16),
            pltpu.VMEM((rows, rows), BF16),
            pltpu.VMEM((rows // 2, rows // 2), BF16),
            pltpu.VMEM((2 * nz, 2 * nz), BF16),
            pltpu.VMEM((rows, 2 * nz), BF16),
            pltpu.VMEM((chunks, rows, 2 * nz), BF16),
            pltpu.VMEM((chunks, n_snap, part, 2 * nz), BF16),
            pltpu.VMEM((2 * total, 3 * total), BF16),
            pltpu.VMEM((total, wide), F32),
            pltpu.VMEM((n_space, tile_rows, wide), F32),
            pltpu.VMEM((tile_rows, wide), F32),
            pltpu.VMEM((n_snap - 1, tile_rows, wide), F32),
            dma((4,)),
            dma((2, 2)),
            dma((2, 2)),
            dma((chunks, n_snap - 1)),
            dma((chunks, n_snap - 1)),
            dma((n_space - 1,)),
            dma((n_space - 1,)),
            dma((n_snap - 1,)),
            dma((n_snap - 1,)),
        ],
        compiler_params=pltpu.CompilerParams(
            collective_id=0, has_side_effects=True, vmem_limit_bytes=62 * 1024 * 1024
        ),
        cost_estimate=pl.CostEstimate(
            flops=4_000_000_000, bytes_accessed=4_000_000, transcendentals=0
        ),
    )(tile_owner, phase_bins.reshape(1, total), velocity)


def solution(mesh):
    return jax.shard_map(
        per_device,
        mesh=mesh,
        in_specs=(P("snap", None, "space", None, None), P(), P()),
        out_specs=P("space", None, "snap"),
        check_vma=False,
    )
```

```python
import functools
import jax
import jax.numpy as jnp
from jax import lax
from jax.experimental import pallas as pl
from jax.experimental.pallas import tpu as pltpu
from jax.sharding import PartitionSpec as P

NB = 24
MESH = pl.DeviceIdType.MESH
F32 = jnp.float32
BF16 = jnp.bfloat16
HIGH = lax.Precision.HIGHEST


def iota2(shape, dim):
    return lax.broadcasted_iota(jnp.int32, shape, dim)


def stencil(step):
    plus = jnp.where(step == 1, 8.0, 0.0) - jnp.where(step == 2, 1.0, 0.0)
    minus = jnp.where(step == -1, 8.0, 0.0) - jnp.where(step == -2, 1.0, 0.0)
    return plus - minus


def kernel(
    n_space, n_snap, inv_voxels,
    owner_hbm, bins_hbm, vel_ref, out_ref,
    owner_ref, bins_ref, ext, uu, perm, band_y, band_z, omega, send, recv, terms, weights, mail, rows_in, cols_out, cols_in,
    local_sem, halo_send, halo_recv, a2a_send, a2a_recv, row_send, row_recv, col_send, col_recv,
):
    snaps, _, nx, ny, nz = vel_ref.shape
    total = snaps * n_snap
    half = snaps * ny // 2
    rows = snaps * ny
    part = rows // n_snap
    y_part = ny // n_snap
    pairs = nx // 2
    tile_rows = total // n_space
    chunks = 3 * pairs
    si = lax.axis_index("space")
    ti = lax.axis_index("snap")

    load_vw = pltpu.make_async_copy(vel_ref.at[:, 1:3], ext.at[:, :, 2 : nx + 2], local_sem.at[0])
    load_u = pltpu.make_async_copy(vel_ref.at[:, 0], uu, local_sem.at[1])
    load_bins = pltpu.make_async_copy(bins_hbm, bins_ref, local_sem.at[2])
    load_owner = pltpu.make_async_copy(owner_hbm, owner_ref, local_sem.at[3])
    load_vw.start()
    load_u.start()
    load_bins.start()
    load_owner.start()

    barrier = pltpu.get_barrier_semaphore()
    for o in range(1, n_snap):
        pl.semaphore_signal(
            barrier, inc=1, device_id={"snap": lax.rem(ti + o, n_snap)}, device_id_type=MESH
        )
    for o in range(1, n_space):
        pl.semaphore_signal(
            barrier, inc=1, device_id={"space": lax.rem(si + o, n_space)}, device_id_type=MESH
        )

    c = iota2((1, rows), 1)
    moved_to = (c % ny) * snaps + c // ny
    perm[...] = jnp.where(iota2((rows, rows), 0) == moved_to, 1.0, 0.0).astype(BF16)

    def band(size, length):
        r = iota2((size, size), 0)
        c = iota2((size, size), 1)
        first = (iota2((1, size), 1) // length) * length
        return jnp.where((r >= first) & (r < first + length), stencil(r - c), 0.0)

    band_y[...] = (-band(half, ny)).astype(BF16)
    band_z[...] = band(2 * nz, nz).astype(BF16)
    mail[...] = jnp.zeros_like(mail)

    def to_left(comp):
        return pltpu.make_async_remote_copy(
            vel_ref.at[:, comp + 1, 0:2], ext.at[:, comp, nx + 2 : nx + 4],
            halo_send.at[0, comp], halo_recv.at[0, comp],
            device_id={"space": si - 1}, device_id_type=MESH,
        )

    def to_right(comp):
        return pltpu.make_async_remote_copy(
            vel_ref.at[:, comp + 1, nx - 2 : nx], ext.at[:, comp, 0:2],
            halo_send.at[1, comp], halo_recv.at[1, comp],
            device_id={"space": si + 1}, device_id_type=MESH,
        )

    @pl.when(si == 0)
    def _():
        ext[:, :, 0:2] = jnp.zeros((snaps, 2, 2, ny, nz), BF16)

    @pl.when(si == n_space - 1)
    def _():
        ext[:, :, nx + 2 : nx + 4] = jnp.zeros((snaps, 2, 2, ny, nz), BF16)

    order = sorted(range(1, n_snap), key=lambda o: abs(o - n_snap // 2))

    def a2a(k, o):
        dst = lax.rem(ti + o, n_snap)
        return pltpu.make_async_remote_copy(
            send.at[k, pl.ds(pl.multiple_of(dst * part, part), part)],
            recv.at[k, ti],
            a2a_send.at[k, o - 1], a2a_recv.at[k, o - 1],
            device_id={"snap": dst}, device_id_type=MESH,
        )

    def arrange(k):
        moved = jnp.dot(perm[...], omega[...], preferred_element_type=F32)
        send[k] = moved.astype(BF16)

    def ship(k):
        for o in order:
            a2a(k, o).start()
        recv[k, ti] = send[k, pl.ds(pl.multiple_of(ti * part, part), part)]

    h_snaps = snaps // 2

    def pair_vw(comp, x, h):
        s = slice(h * h_snaps, (h + 1) * h_snaps)
        return jnp.concatenate(
            [ext[s, comp, x + 2 + i].reshape(half, nz) for i in range(2)], axis=1
        )

    def pair_u(x, h):
        s = slice(h * h_snaps, (h + 1) * h_snaps)
        return jnp.concatenate([uu[s, x + i].reshape(half, nz) for i in range(2)], axis=1)

    def d1_pair(comp, x, h):
        s = slice(h * h_snaps, (h + 1) * h_snaps)
        f = [ext[s, comp, x + i].reshape(half, nz).astype(F32) for i in range(6)]
        return jnp.concatenate(
            [8.0 * (f[i + 3] - f[i + 1]) - (f[i + 4] - f[i]) for i in range(2)], axis=1
        )

    def d2(field):
        return jnp.dot(band_y[...], field, preferred_element_type=F32)

    def d3(field):
        return jnp.dot(field, band_z[...], preferred_element_type=F32)

    def put(h, value):
        omega[h * half : (h + 1) * half] = (value * (1.0 / 12.0)).astype(BF16)

    def make_x(k, x):
        for h in range(2):
            put(h, d2(pair_vw(1, x, h)) - d3(pair_vw(0, x, h)))
        arrange(k)

    def make_y(k, x):
        for h in range(2):
            put(h, d3(pair_u(x, h)) - d1_pair(1, x, h))
        arrange(k)

    def make_z(k, x):
        for h in range(2):
            put(h, d1_pair(0, x, h) - d2(pair_u(x, h)))
        arrange(k)

    load_vw.wait()
    make_x(0, 0)

    pl.semaphore_wait(barrier, n_snap + n_space - 2)
    ship(0)

    def start_halo(comp):
        @pl.when(si > 0)
        def _():
            to_left(comp).start()

        @pl.when(si < n_space - 1)
        def _():
            to_right(comp).start()

    start_halo(1)

    def x_step(p, _):
        make_x(p, 2 * p)
        ship(p)
        return 0

    lax.fori_loop(1, pairs, x_step, 0)
    start_halo(0)
    load_u.wait()

    def inner(p, _):
        k = pairs + 2 * p
        make_y(k, 2 * p + 2)
        ship(k)
        make_z(k + 1, 2 * p + 2)
        ship(k + 1)
        return 0

    lax.fori_loop(0, pairs - 2, inner, 0)

    load_bins.wait()
    load_owner.wait()
    onehot = jnp.where(bins_ref[...] == iota2((32, total), 0), 1.0, 0.0).astype(F32)
    same = lax.dot_general(
        onehot, onehot, (((0,), (0,)), ((), ())), preferred_element_type=F32
    )
    averaging = same / jnp.sum(same, axis=0, keepdims=True)
    r = iota2((total, total), 0)
    c = iota2((total, total), 1)
    centre = jnp.where(r == c, 1.0, 0.0) - averaging
    c1 = iota2((1, total), 1)
    tile = c1 // tile_rows
    first_row = jnp.zeros((1, total), jnp.int32)
    for t in range(n_space):
        first_row = jnp.where(tile == t, owner_ref[t] * tile_rows, first_row)
    place = jnp.where(r == first_row + c1 % tile_rows, 1.0, 0.0)
    rest = jnp.concatenate(
        [centre, jnp.dot(place, centre, preferred_element_type=F32, precision=HIGH)], axis=0
    )
    for term in range(3):
        terms[term] = rest.astype(BF16)
        rest = rest - terms[term].astype(F32)
    weights[...] = jnp.concatenate(
        [terms[term].astype(F32) for term in range(3)], axis=1
    ).astype(BF16)

    def accumulate(k, _):
        for o in order:
            a2a(k, o).wait_recv()
        columns = jnp.concatenate(
            [
                jnp.concatenate(
                    [recv[k, t, y * snaps : (y + 1) * snaps] for t in range(n_snap)], axis=0
                )
                for y in range(y_part)
            ],
            axis=1,
        )
        near = jnp.dot(
            weights[...], jnp.concatenate([columns] * 3, axis=0), preferred_element_type=F32
        ).astype(BF16)
        mail[:, 0:total] += lax.dot_general(
            near[total:], near[:total], (((1,), (1,)), ((), ())), preferred_element_type=F32
        )
        return 0

    def edges(comp, make, base):
        @pl.when(si < n_space - 1)
        def _():
            to_left(comp).wait_recv()

        @pl.when(si > 0)
        def _():
            to_right(comp).wait_recv()

        def side(p, _):
            make(base + p, p * (nx - 2))
            ship(base + p)
            return 0

        lax.fori_loop(0, 2, side, 0)

    lax.fori_loop(0, 2, accumulate, 0)
    edges(1, make_y, chunks - 4)
    lax.fori_loop(2, 4, accumulate, 0)
    edges(0, make_z, chunks - 2)
    lax.fori_loop(4, chunks, accumulate, 0)

    def row_copy(o):
        dst = lax.rem(si + o, n_space)
        return pltpu.make_async_remote_copy(
            mail.at[pl.ds(pl.multiple_of(dst * tile_rows, tile_rows), tile_rows)],
            rows_in.at[si], row_send.at[o - 1], row_recv.at[o - 1],
            device_id={"space": dst}, device_id_type=MESH,
        )

    for o in sorted(range(1, n_space), key=lambda o: abs(o - n_space // 2)):
        row_copy(o).start()
    rows_in[si] = mail[pl.ds(pl.multiple_of(si * tile_rows, tile_rows), tile_rows)]
    for o in range(1, n_space):
        row_copy(o).wait_recv()
    mine = jnp.sum(rows_in[...], axis=0) * inv_voxels
    cols_out[...] = mine

    def col_copy(o):
        return pltpu.make_async_remote_copy(
            cols_out, cols_in.at[o - 1], col_send.at[o - 1], col_recv.at[o - 1],
            device_id={"snap": lax.rem(ti + o, n_snap)}, device_id_type=MESH,
        )

    for o in order:
        col_copy(o).start()
    for o in order:
        col_copy(o).wait_recv()
    summed = mine + jnp.sum(cols_in[...], axis=0)
    wide = summed.shape[1]
    turned = pltpu.roll(summed, lax.rem(wide - ti * snaps, wide), 1)
    out_ref[0] = turned[:, 0:snaps]

    def drain(k, _):
        for o in order:
            a2a(k, o).wait_send()
        return 0

    lax.fori_loop(0, chunks, drain, 0)

    for comp in range(2):
        @pl.when(si > 0)
        def _():
            to_left(comp).wait_send()

        @pl.when(si < n_space - 1)
        def _():
            to_right(comp).wait_send()

    for o in range(1, n_space):
        row_copy(o).wait_send()
    for o in order:
        col_copy(o).wait_send()


def per_device(velocity, phase_bins, tile_owner):
    n_space = lax.axis_size("space")
    n_snap = lax.axis_size("snap")
    snaps, _, nx, ny, nz = velocity.shape
    total = snaps * n_snap
    rows = snaps * ny
    part = rows // n_snap
    chunks = 3 * (nx // 2)
    tile_rows = total // n_space
    wide = -(-total // 128) * 128
    dma = pltpu.SemaphoreType.DMA
    return pl.pallas_call(
        functools.partial(kernel, n_space, n_snap, 1.0 / (n_space * nx * ny * nz)),
        out_shape=jax.ShapeDtypeStruct((1, tile_rows, snaps), F32),
        in_specs=[
            pl.BlockSpec(memory_space=pltpu.HBM),
            pl.BlockSpec(memory_space=pltpu.HBM),
            pl.BlockSpec(memory_space=pltpu.HBM),
        ],
        out_specs=pl.BlockSpec(memory_space=pltpu.VMEM),
        scratch_shapes=[
            pltpu.SMEM((n_space,), jnp.int32),
            pltpu.VMEM((1, total), jnp.int32),
            pltpu.VMEM((snaps, 2, nx + 4, ny, nz), BF16),
            pltpu.VMEM((snaps, nx, ny, nz), BF16),
            pltpu.VMEM((rows, rows), BF16),
            pltpu.VMEM((rows // 2, rows // 2), BF16),
            pltpu.VMEM((2 * nz, 2 * nz), BF16),
            pltpu.VMEM((rows, 2 * nz), BF16),
            pltpu.VMEM((chunks, rows, 2 * nz), BF16),
            pltpu.VMEM((chunks, n_snap, part, 2 * nz), BF16),
            pltpu.VMEM((3, 2 * total, total), BF16),
            pltpu.VMEM((2 * total, 3 * total), BF16),
            pltpu.VMEM((total, wide), F32),
            pltpu.VMEM((n_space, tile_rows, wide), F32),
            pltpu.VMEM((tile_rows, wide), F32),
            pltpu.VMEM((n_snap - 1, tile_rows, wide), F32),
            dma((4,)),
            dma((2, 2)),
            dma((2, 2)),
            dma((chunks, n_snap - 1)),
            dma((chunks, n_snap - 1)),
            dma((n_space - 1,)),
            dma((n_space - 1,)),
            dma((n_snap - 1,)),
            dma((n_snap - 1,)),
        ],
        compiler_params=pltpu.CompilerParams(
            collective_id=0, has_side_effects=True, vmem_limit_bytes=61952 * 1024
        ),
        cost_estimate=pl.CostEstimate(
            flops=4_000_000_000, bytes_accessed=4_000_000, transcendentals=0
        ),
    )(tile_owner, phase_bins.reshape(1, total), velocity)


def solution(mesh):
    return jax.shard_map(
        per_device,
        mesh=mesh,
        in_specs=(P("snap", None, "space", None, None), P(), P()),
        out_specs=P("space", None, "snap"),
        check_vma=False,
    )
```

```python
import functools
import jax
import jax.numpy as jnp
from jax import lax
from jax.experimental import pallas as pl
from jax.experimental.pallas import tpu as pltpu
from jax.sharding import PartitionSpec as P

NB = 24
MESH = pl.DeviceIdType.MESH
F32 = jnp.float32
BF16 = jnp.bfloat16
HIGH = lax.Precision.HIGHEST


def iota2(shape, dim):
    return lax.broadcasted_iota(jnp.int32, shape, dim)


def stencil(step):
    plus = jnp.where(step == 1, 8.0, 0.0) - jnp.where(step == 2, 1.0, 0.0)
    minus = jnp.where(step == -1, 8.0, 0.0) - jnp.where(step == -2, 1.0, 0.0)
    return plus - minus


def kernel(
    n_space, n_snap, inv_voxels,
    owner_hbm, bins_hbm, vel_ref, out_ref,
    owner_ref, bins_ref, ext, uu, perm, band_y, band_z, omega, send, recv, mean_mat, centre_mat, left_mat, gram, mail, rows_in, cols_out, cols_in,
    local_sem, halo_send, halo_recv, a2a_send, a2a_recv, row_send, row_recv, col_send, col_recv,
):
    snaps, _, nx, ny, nz = vel_ref.shape
    total = snaps * n_snap
    half = snaps * ny // 2
    rows = snaps * ny
    part = rows // n_snap
    y_part = ny // n_snap
    pairs = nx // 2
    tile_rows = total // n_space
    chunks = 3 * pairs
    si = lax.axis_index("space")
    ti = lax.axis_index("snap")

    load_first = pltpu.make_async_copy(vel_ref.at[:, 1:3, 0:2], ext.at[:, :, 2:4], local_sem.at[4])
    load_vw = pltpu.make_async_copy(
        vel_ref.at[:, 1:3, 2:nx], ext.at[:, :, 4 : nx + 2], local_sem.at[0]
    )
    load_first.start()
    load_u = pltpu.make_async_copy(vel_ref.at[:, 0], uu, local_sem.at[1])
    load_bins = pltpu.make_async_copy(bins_hbm, bins_ref, local_sem.at[2])
    load_owner = pltpu.make_async_copy(owner_hbm, owner_ref, local_sem.at[3])
    load_vw.start()
    load_u.start()
    load_bins.start()
    load_owner.start()

    barrier = pltpu.get_barrier_semaphore()
    for o in range(1, n_snap):
        pl.semaphore_signal(
            barrier, inc=1, device_id={"snap": lax.rem(ti + o, n_snap)}, device_id_type=MESH
        )
    for o in range(1, n_space):
        pl.semaphore_signal(
            barrier, inc=1, device_id={"space": lax.rem(si + o, n_space)}, device_id_type=MESH
        )

    c = iota2((1, rows), 1)
    moved_to = (c % ny) * snaps + c // ny
    perm[...] = jnp.where(iota2((rows, rows), 0) == moved_to, 1.0, 0.0).astype(BF16)

    def band(size, length):
        r = iota2((size, size), 0)
        c = iota2((size, size), 1)
        first = (iota2((1, size), 1) // length) * length
        return jnp.where((r >= first) & (r < first + length), stencil(r - c), 0.0)

    band_y[...] = (-band(half, ny)).astype(BF16)
    band_z[...] = band(2 * nz, nz).astype(BF16)
    gram[...] = jnp.zeros_like(gram)

    def to_left(comp):
        return pltpu.make_async_remote_copy(
            vel_ref.at[:, comp + 1, 0:2], ext.at[:, comp, nx + 2 : nx + 4],
            halo_send.at[0, comp], halo_recv.at[0, comp],
            device_id={"space": si - 1}, device_id_type=MESH,
        )

    def to_right(comp):
        return pltpu.make_async_remote_copy(
            vel_ref.at[:, comp + 1, nx - 2 : nx], ext.at[:, comp, 0:2],
            halo_send.at[1, comp], halo_recv.at[1, comp],
            device_id={"space": si + 1}, device_id_type=MESH,
        )

    @pl.when(si == 0)
    def _():
        ext[:, :, 0:2] = jnp.zeros((snaps, 2, 2, ny, nz), BF16)

    @pl.when(si == n_space - 1)
    def _():
        ext[:, :, nx + 2 : nx + 4] = jnp.zeros((snaps, 2, 2, ny, nz), BF16)

    order = sorted(range(1, n_snap), key=lambda o: abs(o - n_snap // 2))

    def a2a(k, o):
        dst = lax.rem(ti + o, n_snap)
        return pltpu.make_async_remote_copy(
            send.at[k, pl.ds(pl.multiple_of(dst * part, part), part)],
            recv.at[k, ti],
            a2a_send.at[k, o - 1], a2a_recv.at[k, o - 1],
            device_id={"snap": dst}, device_id_type=MESH,
        )

    def arrange(k):
        moved = jnp.dot(perm[...], omega[...], preferred_element_type=F32)
        send[k] = moved.astype(BF16)

    def ship(k):
        for o in order:
            a2a(k, o).start()
        recv[k, ti] = send[k, pl.ds(pl.multiple_of(ti * part, part), part)]

    h_snaps = snaps // 2

    def pair_vw(comp, x, h):
        s = slice(h * h_snaps, (h + 1) * h_snaps)
        return jnp.concatenate(
            [ext[s, comp, x + 2 + i].reshape(half, nz) for i in range(2)], axis=1
        )

    def pair_u(x, h):
        s = slice(h * h_snaps, (h + 1) * h_snaps)
        return jnp.concatenate([uu[s, x + i].reshape(half, nz) for i in range(2)], axis=1)

    def d1_pair(comp, x, h):
        s = slice(h * h_snaps, (h + 1) * h_snaps)
        f = [ext[s, comp, x + i].reshape(half, nz).astype(F32) for i in range(6)]
        return jnp.concatenate(
            [8.0 * (f[i + 3] - f[i + 1]) - (f[i + 4] - f[i]) for i in range(2)], axis=1
        )

    def d2(field):
        return jnp.dot(band_y[...], field, preferred_element_type=F32)

    def d3(field):
        return jnp.dot(field, band_z[...], preferred_element_type=F32)

    def put(h, value):
        omega[h * half : (h + 1) * half] = (value * (1.0 / 12.0)).astype(BF16)

    def make_x(k, x):
        for h in range(2):
            put(h, d2(pair_vw(1, x, h)) - d3(pair_vw(0, x, h)))
        arrange(k)

    def make_y(k, x):
        for h in range(2):
            put(h, d3(pair_u(x, h)) - d1_pair(1, x, h))
        arrange(k)

    def make_z(k, x):
        for h in range(2):
            put(h, d1_pair(0, x, h) - d2(pair_u(x, h)))
        arrange(k)

    load_first.wait()
    make_x(0, 0)

    pl.semaphore_wait(barrier, n_snap + n_space - 2)
    ship(0)
    for comp in (1, 0):
        @pl.when(si > 0)
        def _():
            to_left(comp).start()

        @pl.when(si < n_space - 1)
        def _():
            to_right(comp).start()

    load_vw.wait()

    def x_step(p, _):
        make_x(p, 2 * p)
        ship(p)
        return 0

    lax.fori_loop(1, pairs, x_step, 0)
    load_u.wait()

    def inner(p, _):
        k = pairs + 2 * p
        make_y(k, 2 * p + 2)
        ship(k)
        make_z(k + 1, 2 * p + 2)
        ship(k + 1)
        return 0

    lax.fori_loop(0, pairs - 2, inner, 0)

    load_bins.wait()
    load_owner.wait()
    onehot = jnp.where(bins_ref[...] == iota2((32, total), 0), 1.0, 0.0).astype(F32)
    same = lax.dot_general(
        onehot, onehot, (((0,), (0,)), ((), ())), preferred_element_type=F32
    )
    averaging = same / jnp.sum(same, axis=0, keepdims=True)
    mean_mat[...] = averaging.astype(BF16)
    r = iota2((total, total), 0)
    c = iota2((total, total), 1)
    centre = jnp.where(r == c, 1.0, 0.0) - averaging
    centre_mat[...] = centre
    c1 = iota2((1, total), 1)
    tile = c1 // tile_rows
    first_row = jnp.zeros((1, total), jnp.int32)
    for t in range(n_space):
        first_row = jnp.where(tile == t, owner_ref[t] * tile_rows, first_row)
    place = jnp.where(r == first_row + c1 % tile_rows, inv_voxels, 0.0)
    left_mat[...] = jnp.dot(place, centre, preferred_element_type=F32, precision=HIGH)

    def accumulate(k, _):
        for o in order:
            a2a(k, o).wait_recv()
        columns = jnp.concatenate(
            [
                jnp.concatenate(
                    [recv[k, t, y * snaps : (y + 1) * snaps] for t in range(n_snap)], axis=0
                )
                for y in range(y_part)
            ],
            axis=1,
        )
        mean = jnp.dot(mean_mat[...], columns, preferred_element_type=F32)
        near = (columns.astype(F32) - mean).astype(BF16)
        gram[...] += lax.dot_general(
            near, near, (((1,), (1,)), ((), ())), preferred_element_type=F32
        )
        return 0

    def edges(comp, make, base):
        @pl.when(si < n_space - 1)
        def _():
            to_left(comp).wait_recv()

        @pl.when(si > 0)
        def _():
            to_right(comp).wait_recv()

        def side(p, _):
            make(base + p, p * (nx - 2))
            ship(base + p)
            return 0

        lax.fori_loop(0, 2, side, 0)

    lax.fori_loop(0, 2, accumulate, 0)
    edges(1, make_y, chunks - 4)
    lax.fori_loop(2, 4, accumulate, 0)
    edges(0, make_z, chunks - 2)
    lax.fori_loop(4, chunks, accumulate, 0)

    lines = jnp.dot(left_mat[...], gram[...], preferred_element_type=F32, precision=HIGH)
    done = jnp.dot(lines, centre_mat[...], preferred_element_type=F32, precision=HIGH)
    mail[...] = jnp.zeros_like(mail)
    mail[:, 0:total] = done

    def row_copy(o):
        dst = lax.rem(si + o, n_space)
        return pltpu.make_async_remote_copy(
            mail.at[pl.ds(pl.multiple_of(dst * tile_rows, tile_rows), tile_rows)],
            rows_in.at[si], row_send.at[o - 1], row_recv.at[o - 1],
            device_id={"space": dst}, device_id_type=MESH,
        )

    for o in range(1, n_space):
        row_copy(o).start()
    rows_in[si] = mail[pl.ds(pl.multiple_of(si * tile_rows, tile_rows), tile_rows)]
    for o in range(1, n_space):
        row_copy(o).wait_recv()
    mine = jnp.sum(rows_in[...], axis=0)
    cols_out[...] = mine

    def col_copy(o):
        return pltpu.make_async_remote_copy(
            cols_out, cols_in.at[o - 1], col_send.at[o - 1], col_recv.at[o - 1],
            device_id={"snap": lax.rem(ti + o, n_snap)}, device_id_type=MESH,
        )

    for o in order:
        col_copy(o).start()
    for o in order:
        col_copy(o).wait_recv()
    out_ref[...] = mine + jnp.sum(cols_in[...], axis=0)

    def drain(k, _):
        for o in order:
            a2a(k, o).wait_send()
        return 0

    lax.fori_loop(0, chunks, drain, 0)

    for comp in range(2):
        @pl.when(si > 0)
        def _():
            to_left(comp).wait_send()

        @pl.when(si < n_space - 1)
        def _():
            to_right(comp).wait_send()

    for o in range(1, n_space):
        row_copy(o).wait_send()
    for o in order:
        col_copy(o).wait_send()


def per_device(velocity, phase_bins, tile_owner):
    n_space = lax.axis_size("space")
    n_snap = lax.axis_size("snap")
    snaps, _, nx, ny, nz = velocity.shape
    total = snaps * n_snap
    rows = snaps * ny
    part = rows // n_snap
    chunks = 3 * (nx // 2)
    tile_rows = total // n_space
    wide = -(-total // 128) * 128
    dma = pltpu.SemaphoreType.DMA
    summed = pl.pallas_call(
        functools.partial(kernel, n_space, n_snap, 1.0 / (n_space * nx * ny * nz)),
        out_shape=jax.ShapeDtypeStruct((tile_rows, wide), F32),
        in_specs=[
            pl.BlockSpec(memory_space=pl.ANY),
            pl.BlockSpec(memory_space=pl.ANY),
            pl.BlockSpec(memory_space=pl.ANY),
        ],
        out_specs=pl.BlockSpec(memory_space=pltpu.VMEM),
        scratch_shapes=[
            pltpu.SMEM((n_space,), jnp.int32),
            pltpu.VMEM((1, total), jnp.int32),
            pltpu.VMEM((snaps, 2, nx + 4, ny, nz), BF16),
            pltpu.VMEM((snaps, nx, ny, nz), BF16),
            pltpu.VMEM((rows, rows), BF16),
            pltpu.VMEM((rows // 2, rows // 2), BF16),
            pltpu.VMEM((2 * nz, 2 * nz), BF16),
            pltpu.VMEM((rows, 2 * nz), BF16),
            pltpu.VMEM((chunks, rows, 2 * nz), BF16),
            pltpu.VMEM((chunks, n_snap, part, 2 * nz), BF16),
            pltpu.VMEM((total, total), BF16),
            pltpu.VMEM((total, total), F32),
            pltpu.VMEM((total, total), F32),
            pltpu.VMEM((total, total), F32),
            pltpu.VMEM((total, wide), F32),
            pltpu.VMEM((n_space, tile_rows, wide), F32),
            pltpu.VMEM((tile_rows, wide), F32),
            pltpu.VMEM((n_snap - 1, tile_rows, wide), F32),
            dma((5,)),
            dma((2, 2)),
            dma((2, 2)),
            dma((chunks, n_snap - 1)),
            dma((chunks, n_snap - 1)),
            dma((n_space - 1,)),
            dma((n_space - 1,)),
            dma((n_snap - 1,)),
            dma((n_snap - 1,)),
        ],
        compiler_params=pltpu.CompilerParams(
            collective_id=0, has_side_effects=True, vmem_limit_bytes=62 * 1024 * 1024
        ),
        cost_estimate=pl.CostEstimate(
            flops=4_000_000_000, bytes_accessed=4_000_000, transcendentals=0
        ),
    )(tile_owner, phase_bins.reshape(1, total), velocity)
    return lax.dynamic_slice_in_dim(summed, lax.axis_index("snap") * snaps, snaps, axis=1)[None]


def solution(mesh):
    return jax.shard_map(
        per_device,
        mesh=mesh,
        in_specs=(P("snap", None, "space", None, None), P(), P()),
        out_specs=P("space", None, "snap"),
        check_vma=False,
    )
```
